32 devices in a mesh: depth: 2 (over x), row: 4 (over y, core), col: 4 (over z).
Axes of the slice: x: 2, y: 2, z: 4, core: 2. Of those that a mesh axis runs over, the one named last changes fastest.
Arguments:
- hidden: bfloat16 [512, 28672], P('col', ('depth', 'row')), may hold values from -6 to 6
- upstream: bfloat16 [512, 14336], P(('depth', 'row'), 'col'), may hold values from -6 to 6
- weight: bfloat16 [28672, 14336], P(('depth', 'row'), 'col'), may hold values from -0.03125 to 0.03125
Outputs:
- input_grad: bfloat16 [512, 28672], P('col', ('depth', 'row'))
- weight_grad: bfloat16 [28672, 14336], P(('depth', 'row'), 'col')
The draws below stay inside these ranges and needn't reach their ends.
All inputs are finite; a program needn't handle non-finite values.
Results may differ from the reference program's by a relative error of at most 0.012.
Values may be sent and summed in bfloat16 or wider, within the bound.
A program may use at most 192 MiB of HBM per device.

```python
import math
import jax
import jax.numpy as jnp
from jax import lax

D = 14336
FF = 28672
TOKENS = 512
N_COL = 4


def level_of(own_key, extent, pieces, low, largest):
    def one(axis_at, parts):
        draws = jax.random.uniform(jax.random.fold_in(jax.random.fold_in(own_key, 6), axis_at), (parts,), jnp.float32, low / len(pieces), largest / len(pieces))
        return jnp.repeat(jnp.exp(draws), extent[axis_at] // parts).reshape((-1,) + (1,) * (len(extent) - axis_at - 1))

    loudness = one(*pieces[0])
    for cut in pieces[1:]:
        loudness = loudness * one(*cut)
    return loudness


def normal_values(rng, extent, deviation, limit, shards=(), held_as=jnp.bfloat16):
    drawn = jax.random.normal(rng, extent, jnp.float32) * deviation
    if len(shards) > 0:
        drawn = level_of(rng, extent, shards, -0.22, 0.18) * drawn
    return jnp.clip(drawn, min=-limit, max=limit).astype(held_as)


def setup_inputs(seed: int = 0) -> dict:
    streams_of = jax.random.split(jax.random.key(seed), 4)
    hidden = normal_values(streams_of[0], (TOKENS, FF), 1.0, 6.0, ((0, 4), (1, 8)))
    upstream = normal_values(streams_of[1], (TOKENS, D), 1.0, 6.0, ((0, 8), (1, 4)))
    weight = normal_values(streams_of[2], (FF, D), FF ** -0.5, 0.03125, ((0, 8), (1, 4)))
    return {"hidden": hidden, "upstream": upstream, "weight": weight}


def reference(hidden, upstream, weight):
    block_rows = math.gcd(FF, 1024)
    count_blocks = FF // block_rows
    feature_block = D // N_COL
    token_scale = 1.0 / math.sqrt(TOKENS)
    upstream_wide = upstream.astype(jnp.float32)
    upstream_split = upstream_wide.reshape(TOKENS, N_COL, feature_block)
    weight_blocks = weight.reshape(count_blocks, block_rows, D)
    hidden_blocks = hidden.T.reshape(count_blocks, block_rows, TOKENS)

    def per_block(block_pair):
        weight_piece, hidden_piece = block_pair
        weight_wide = weight_piece.astype(jnp.float32).reshape(block_rows, N_COL, feature_block)
        partials = jnp.einsum('tcd,fcd->ctf', upstream_split, weight_wide, precision=lax.Precision.HIGHEST)
        partials = partials.astype(jnp.bfloat16).astype(jnp.float32)
        grad_input = lax.optimization_barrier(jnp.sum(partials, axis=0))
        grad_weight = jnp.dot(hidden_piece.astype(jnp.float32), upstream_wide, precision=lax.Precision.HIGHEST)
        grad_weight = grad_weight * token_scale
        return (grad_input.astype(jnp.bfloat16), grad_weight.astype(jnp.bfloat16))
    grad_inputs, grad_weights = lax.map(per_block, (weight_blocks, hidden_blocks))
    input_grad = grad_inputs.transpose(1, 0, 2).reshape(TOKENS, FF)
    weight_grad = grad_weights.reshape(FF, D)
    return (input_grad, weight_grad)
```

```python
import functools
import math

import jax
import jax.numpy as jnp
from jax import lax
from jax.experimental import pallas as pl
from jax.experimental.pallas import tpu as pltpu
from jax.sharding import PartitionSpec as P

MESH = pl.DeviceIdType.MESH
HALVES = 2
LAG = 2
VMEM_BYTES = 60 * 1024 * 1024


def exchange_kernel(
    sizes, hid, up, w, hall, uall, own, to_right, to_left,
    up_all, w_all, part, got,
    up_local, hid_local, w_sem, out_sem,
    up_send, up_recv, fwd_send, fwd_recv,
    ag_send, ag_recv, rs_send, rs_recv,
):
    n, depth_n, row_n, chunks = sizes
    group = depth_n * row_n
    pairs = group // 2
    rows = hid.shape[0]
    up_rows = up.shape[0]
    unit = part.shape[2]
    half = rows // HALVES
    depth, row, z = lax.axis_index("depth"), lax.axis_index("row"), lax.axis_index("col")
    me = depth * row_n + row
    partner = me + 1 - 2 * lax.rem(me, 2)

    def plane(i):
        return (lax.div(i, row_n), lax.rem(i, row_n), z)

    def line(way):
        return (depth, row, jnp.clip(z + (1 - 2 * way), 0, n - 1))

    place = (z, n - 1 - z)

    def block_of(way, e):
        return e if way == 0 else n - 1 - e

    barrier = pltpu.get_barrier_semaphore()
    for k in range(1, pairs):
        pl.semaphore_signal(barrier, inc=1, device_id=plane(lax.rem(me + 2 * k, group)), device_id_type=MESH)
    pl.semaphore_signal(barrier, inc=1, device_id=plane(partner), device_id_type=MESH)
    for way in range(2):
        @pl.when(place[way] < n - 1)
        def _():
            pl.semaphore_signal(barrier, inc=1, device_id=line(way), device_id_type=MESH)
    near = jnp.where(z > 0, 1, 0) + jnp.where(z < n - 1, 1, 0)
    pl.semaphore_wait(barrier, pairs + near)

    def up_at(i):
        return up_all.at[pl.ds(pl.multiple_of(i * up_rows, up_rows), up_rows), :]

    def up_copy(k, source):
        return pltpu.make_async_remote_copy(
            src_ref=up, dst_ref=up_at(source), send_sem=up_send.at[k], recv_sem=up_recv.at[k],
            device_id=plane(lax.rem(me + 2 * k, group)), device_id_type=MESH)

    def fwd_copy(k, source, first=False):
        return pltpu.make_async_remote_copy(
            src_ref=up if first else up_at(source), dst_ref=up_at(source),
            send_sem=fwd_send.at[k], recv_sem=fwd_recv.at[k],
            device_id=plane(partner), device_id_type=MESH)

    def hid_rows(ref, b, c):
        return ref.at[pl.ds(pl.multiple_of(b * rows + c * half, half), half), :]

    def ag_copy(way, s, c):
        b = jnp.clip(z - (1 - 2 * way) * (s - 1), 0, n - 1)
        src = hid.at[pl.ds(c * half, half), :] if s == 1 else hid_rows(hall, b, c)
        return pltpu.make_async_remote_copy(
            src_ref=src, dst_ref=hid_rows(hall, b, c),
            send_sem=ag_send.at[way, s - 1, c], recv_sem=ag_recv.at[way, s - 1, c],
            device_id=line(way), device_id_type=MESH)

    def ag_arrive(way, s, c):
        b = jnp.clip(z - (1 - 2 * way) * s, 0, n - 1)
        pltpu.make_async_remote_copy(
            src_ref=hid_rows(hall, b, c), dst_ref=hid_rows(hall, b, c),
            send_sem=ag_send.at[way, s - 1, c], recv_sem=ag_recv.at[way, s - 1, c],
            device_id=line(way), device_id_type=MESH).wait_recv()

    def ag_pass(s, c):
        for way in range(2):
            p = place[way]

            @pl.when(p >= s)
            def _():
                ag_arrive(way, s, c)
                if s + 1 <= n - 1:
                    @pl.when(p < n - 1)
                    def _():
                        ag_copy(way, s + 1, c).start()

    for c in range(HALVES):
        for way in range(2):
            @pl.when(place[way] < n - 1)
            def _():
                ag_copy(way, 1, c).start()
    for k in range(1, pairs):
        up_copy(k, me).start()
    fwd_copy(0, me, True).start()
    own_up = pltpu.make_async_copy(up, up_at(me), up_local)
    own_up.start()
    own_hid = pltpu.make_async_copy(hid, hall.at[pl.ds(pl.multiple_of(z * rows, rows), rows), :], hid_local)
    own_hid.start()

    def w_copy(j):
        return pltpu.make_async_copy(
            w.at[pl.ds(pl.multiple_of(j * unit, unit), unit), :], w_all.at[j], w_sem.at[j])

    for j in range(chunks):
        w_copy(j).start()

    for k in range(1, pairs):
        source = lax.rem(me - 2 * k + group, group)
        up_copy(k, source).wait_recv()
        fwd_copy(k, source).start()
    for c in range(HALVES):
        if n > 1:
            ag_pass(1, c)
    own_up.wait()
    for k in range(pairs):
        fwd_copy(k, lax.rem(partner - 2 * k + group, group)).wait_recv()
    keep_up = pltpu.make_async_copy(up_all, uall, out_sem)
    keep_up.start()

    def part_at(j, b):
        return part.at[j, pl.ds(pl.multiple_of(b * rows, rows), rows), :]

    def rs_copy(way, j, b):
        return pltpu.make_async_remote_copy(
            src_ref=part_at(j, b), dst_ref=got.at[way, j, b],
            send_sem=rs_send.at[way, j, b], recv_sem=rs_recv.at[way, j, b],
            device_id=line(way), device_id_type=MESH)

    def rs_add(way, j, b):
        rs_copy(way, j, b).wait_recv()
        return (part_at(j, b)[...].astype(jnp.float32) + got[way, j, b].astype(jnp.float32)).astype(part.dtype)

    def rs_hop(way, j, e):
        b = block_of(way, e)

        @pl.when(place[way] > 0)
        def _():
            part_at(j, b)[...] = rs_add(way, j, b)
        rs_copy(way, j, b).start()

    later = [(s, c) for s in range(2, n) for c in range(HALVES)]
    slot_of = [min(1 + 3 * i, chunks - 1) for i in range(len(later))]

    @pl.loop(0, chunks)
    def _(j):
        w_copy(j).wait()
        part[j] = lax.dot_general(
            up_all[...], w_all[j], (((1,), (1,)), ((), ())), preferred_element_type=jnp.float32
        ).astype(part.dtype)
        for way in range(2):
            p = place[way]

            @pl.when(p == 0)
            def _():
                if n >= 3:
                    rs_hop(way, j, n - 1)

            @pl.when((p > 0) & (p <= n - 3) & (j >= LAG))
            def _():
                rs_hop(way, j - LAG, n - 1)
        for (s, c), slot in zip(later, slot_of):
            if slot < chunks - 1:
                @pl.when(j == slot)
                def _():
                    ag_pass(s, c)

    for (s, c), slot in zip(later, slot_of):
        if slot >= chunks - 1 and s < n - 1:
            ag_pass(s, c)

    @pl.loop(max(chunks - LAG, 0), chunks)
    def _(j):
        for way in range(2):
            @pl.when((place[way] > 0) & (place[way] <= n - 3))
            def _():
                rs_hop(way, j, n - 1)

    for e in range(n - 2, 1, -1):
        @pl.loop(0, chunks)
        def _(j):
            for way in range(2):
                @pl.when(place[way] <= e - 2)
                def _():
                    rs_hop(way, j, e)

    for j in range(chunks):
        columns = pl.ds(j * unit, unit)
        own[:, columns] = part_at(j, z)[...]
        for way, out in ((0, to_right), (1, to_left)):
            p = place[way]
            b = jnp.clip(z + (1 - 2 * way), 0, n - 1)

            @pl.when((p > 0) & (p < n - 1))
            def _():
                out[:, columns] = rs_add(way, j, b)

            @pl.when((p == 0) | (p == n - 1))
            def _():
                out[:, columns] = part_at(j, b)[...]

    for (s, c), slot in zip(later, slot_of):
        if slot >= chunks - 1 and s == n - 1:
            ag_pass(s, c)

    for k in range(1, pairs):
        up_copy(k, me).wait_send()
    for k in range(pairs):
        fwd_copy(k, lax.rem(me - 2 * k + group, group), k == 0).wait_send()
    for way in range(2):
        for s in range(1, n):
            @pl.when((place[way] >= s - 1) & (place[way] < n - 1))
            def _():
                for c in range(HALVES):
                    ag_copy(way, s, c).wait_send()
        for e in range(2, n):
            @pl.when(place[way] <= e - 2)
            def _():
                @pl.loop(0, chunks)
                def _(j):
                    rs_copy(way, j, block_of(way, e)).wait_send()
    own_hid.wait()
    keep_up.wait()


def exchange(hidden, upstream, weight, n, depth_n, row_n):
    rows, units = hidden.shape
    up_rows, features = upstream.shape
    tokens = rows * n
    chunks = 7 if units % (7 * 128) == 0 else 1
    unit = units // chunks
    group = depth_n * row_n
    half = jnp.bfloat16
    hbm = pl.BlockSpec(memory_space=pl.ANY)
    vmem = pl.BlockSpec(memory_space=pltpu.VMEM)
    small = jax.ShapeDtypeStruct((rows, units), half)
    dma = pltpu.SemaphoreType.DMA
    return pl.pallas_call(
        functools.partial(exchange_kernel, (n, depth_n, row_n, chunks)),
        out_shape=[
            jax.ShapeDtypeStruct((tokens, units), half),
            jax.ShapeDtypeStruct((tokens, features), half),
            small, small, small,
        ],
        in_specs=[hbm, hbm, hbm],
        out_specs=[hbm, hbm, vmem, vmem, vmem],
        scratch_shapes=[
            pltpu.VMEM((tokens, features), half),
            pltpu.VMEM((chunks, unit, features), half),
            pltpu.VMEM((chunks, tokens, unit), half),
            pltpu.VMEM((2, chunks, n, rows, unit), half),
            dma, dma, dma((chunks,)), dma,
            dma((group // 2,)), dma((group // 2,)), dma((group // 2,)), dma((group // 2,)),
            dma((2, n - 1, HALVES)), dma((2, n - 1, HALVES)),
            dma((2, chunks, n)), dma((2, chunks, n)),
        ],
        compiler_params=pltpu.CompilerParams(
            collective_id=0, has_side_effects=True, vmem_limit_bytes=VMEM_BYTES),
        cost_estimate=pl.CostEstimate(
            flops=2 * tokens * units * features, bytes_accessed=2 * units * features, transcendentals=0),
    )(hidden, upstream, weight)


def local(sizes, hidden, upstream, weight):
    n, depth_n, row_n = sizes
    hidden_all, upstream_all, own, to_right, to_left = exchange(hidden, upstream, weight, n, depth_n, row_n)
    from_left = lax.ppermute(to_right, "col", [(i, i + 1) for i in range(n - 1)])
    from_right = lax.ppermute(to_left, "col", [(i + 1, i) for i in range(n - 1)])
    summed_weight = lax.dot_general(
        hidden_all, upstream_all, (((0,), (0,)), ((), ())), preferred_element_type=jnp.float32)
    token_scale = 1.0 / math.sqrt(hidden_all.shape[0])
    weight_grad = (summed_weight * token_scale).astype(jnp.bfloat16)
    wide = jnp.float32
    input_grad = (own.astype(wide) + from_left.astype(wide) + from_right.astype(wide)).astype(jnp.bfloat16)
    return (input_grad, weight_grad)


def solution(mesh):
    sizes = (mesh.shape["col"], mesh.shape["depth"], mesh.shape["row"])
    in_specs = (P("col", ("depth", "row")), P(("depth", "row"), "col"), P(("depth", "row"), "col"))
    out_specs = (P("col", ("depth", "row")), P(("depth", "row"), "col"))
    return jax.shard_map(
        functools.partial(local, sizes), mesh=mesh, in_specs=in_specs, out_specs=out_specs, check_vma=False)
```

```python
import functools
import math

import jax
import jax.numpy as jnp
from jax import lax
from jax.experimental import pallas as pl
from jax.experimental.pallas import tpu as pltpu
from jax.sharding import PartitionSpec as P

MESH = pl.DeviceIdType.MESH
HALVES = 2
LAG = 2
SLOTS = (0, 4)
VMEM_BYTES = 60 * 1024 * 1024


def exchange_kernel(
    sizes, hid, up, w, hall, uall, own, to_right, to_left,
    up_all, w_all, part, got, hid_own,
    up_local, hid_local, w_sem, out_sem,
    x_send, x_recv, y_send, y_recv, turn_send, turn_recv, core_send, core_recv,
    ag_send, ag_recv, rs_send, rs_recv,
):
    n, depth_n, row_n, chunks = sizes
    pair_n = row_n // 2
    rows = hid.shape[0]
    up_rows = up.shape[0]
    unit = part.shape[2]
    half = rows // HALVES
    depth, row, z = lax.axis_index("depth"), lax.axis_index("row"), lax.axis_index("col")
    core, pair = lax.rem(row, 2), lax.div(row, 2)

    def plane(a, b, c):
        return (lax.rem(depth + a, depth_n), 2 * lax.rem(pair + b, pair_n) + c, z)

    def source(a, b, c):
        return lax.rem(depth - a + depth_n, depth_n) * row_n + 2 * lax.rem(pair - b + pair_n, pair_n) + c

    def line(way):
        return (depth, row, jnp.clip(z + (1 - 2 * way), 0, n - 1))

    place = (z, n - 1 - z)

    def block_of(way, e):
        return e if way == 0 else n - 1 - e

    barrier = pltpu.get_barrier_semaphore()
    peers = [plane(a, 0, core) for a in range(1, depth_n)]
    peers += [plane(0, b, core) for b in range(1, pair_n)]
    peers += [plane(0, 0, 1 - core)]
    for peer in peers:
        pl.semaphore_signal(barrier, inc=1, device_id=peer, device_id_type=MESH)
    for way in range(2):
        @pl.when(place[way] < n - 1)
        def _():
            pl.semaphore_signal(barrier, inc=1, device_id=line(way), device_id_type=MESH)
    near = jnp.where(z > 0, 1, 0) + jnp.where(z < n - 1, 1, 0)
    pl.semaphore_wait(barrier, len(peers) + near)

    def up_at(i, first=0, count=None):
        count = up_rows if count is None else count
        return up_all.at[pl.ds(pl.multiple_of(i * up_rows + first, count), count), :]

    def remote(src, dst, send, recv, peer):
        return pltpu.make_async_remote_copy(
            src_ref=src, dst_ref=dst, send_sem=send, recv_sem=recv, device_id=peer, device_id_type=MESH)

    def x_copy(a, i):
        return remote(up, up_at(i), x_send.at[a], x_recv.at[a], plane(a, 0, core))

    def y_copy(b, i):
        return remote(up, up_at(i), y_send.at[b], y_recv.at[b], plane(0, b, core))

    def turn_copy(part_of, a, b, i):
        piece = up_at(i, part_of * (up_rows // 2), up_rows // 2)
        peer = plane(0, b, core) if part_of == 0 else plane(a, 0, core)
        return remote(piece, piece, turn_send.at[part_of, a, b], turn_recv.at[part_of, a, b], peer)

    def core_copy(a, b, i):
        src = up if a == 0 and b == 0 else up_at(i)
        return remote(src, up_at(i), core_send.at[a, b], core_recv.at[a, b], plane(0, 0, 1 - core))

    def hid_rows(ref, b, c):
        return ref.at[pl.ds(pl.multiple_of(b * rows + c * half, half), half), :]

    def ag_copy(way, s, c):
        b = jnp.clip(z - (1 - 2 * way) * (s - 1), 0, n - 1)
        src = hid.at[pl.ds(c * half, half), :] if s == 1 else hid_rows(hall, b, c)
        return pltpu.make_async_remote_copy(
            src_ref=src, dst_ref=hid_rows(hall, b, c),
            send_sem=ag_send.at[way, s - 1, c], recv_sem=ag_recv.at[way, s - 1, c],
            device_id=line(way), device_id_type=MESH)

    def ag_arrive(way, s, c):
        b = jnp.clip(z - (1 - 2 * way) * s, 0, n - 1)
        pltpu.make_async_remote_copy(
            src_ref=hid_rows(hall, b, c), dst_ref=hid_rows(hall, b, c),
            send_sem=ag_send.at[way, s - 1, c], recv_sem=ag_recv.at[way, s - 1, c],
            device_id=line(way), device_id_type=MESH).wait_recv()

    def ag_pass(s, c):
        for way in range(2):
            @pl.when((place[way] >= s) & (place[way] < n - 1))
            def _():
                ag_arrive(way, s, c)
                ag_copy(way, s + 1, c).start()

    for c in range(HALVES):
        for way in range(2):
            @pl.when(place[way] < n - 1)
            def _():
                ag_copy(way, 1, c).start()
    mine = source(0, 0, core)
    for a in range(1, depth_n):
        x_copy(a, mine).start()
    for b in range(1, pair_n):
        y_copy(b, mine).start()
    core_copy(0, 0, mine).start()
    own_up = pltpu.make_async_copy(up, up_at(mine), up_local)
    own_up.start()
    own_hid = pltpu.make_async_copy(hid, hid_own, hid_local)
    own_hid.start()

    def w_copy(j):
        return pltpu.make_async_copy(
            w.at[pl.ds(pl.multiple_of(j * unit, unit), unit), :], w_all.at[j], w_sem.at[j])

    for j in range(chunks):
        w_copy(j).start()

    own_hid.wait()
    keep_hid = pltpu.make_async_copy(
        hid_own, hall.at[pl.ds(pl.multiple_of(z * rows, rows), rows), :], hid_local)
    keep_hid.start()
    for a in range(1, depth_n):
        i = source(a, 0, core)
        x_copy(a, i).wait_recv()
        for b in range(1, pair_n):
            turn_copy(0, a, b, i).start()
        core_copy(a, 0, i).start()
    for b in range(1, pair_n):
        i = source(0, b, core)
        y_copy(b, i).wait_recv()
        for a in range(1, depth_n):
            turn_copy(1, a, b, i).start()
        core_copy(0, b, i).start()
    for c in range(HALVES - 1):
        ag_pass(1, c)
    for a in range(1, depth_n):
        for b in range(1, pair_n):
            i = source(a, b, core)
            turn_copy(0, a, b, i).wait_recv()
            turn_copy(1, a, b, i).wait_recv()
            core_copy(a, b, i).start()
    own_up.wait()
    for a in range(depth_n):
        for b in range(pair_n):
            core_copy(a, b, source(a, b, 1 - core)).wait_recv()
    keep_up = pltpu.make_async_copy(up_all, uall, out_sem)
    keep_up.start()

    def part_at(j, b):
        return part.at[j, pl.ds(pl.multiple_of(b * rows, rows), rows), :]

    def rs_copy(way, j, b):
        return pltpu.make_async_remote_copy(
            src_ref=part_at(j, b), dst_ref=got.at[way, j, b],
            send_sem=rs_send.at[way, j, b], recv_sem=rs_recv.at[way, j, b],
            device_id=line(way), device_id_type=MESH)

    def rs_add(way, j, b):
        rs_copy(way, j, b).wait_recv()
        return (part_at(j, b)[...].astype(jnp.float32) + got[way, j, b].astype(jnp.float32)).astype(part.dtype)

    def rs_hop(way, j, e):
        b = block_of(way, e)

        @pl.when(place[way] > 0)
        def _():
            part_at(j, b)[...] = rs_add(way, j, b)
        rs_copy(way, j, b).start()

    later = [(1, HALVES - 1)] + [(s, c) for s in range(2, n - 1) for c in range(HALVES)]
    slot_of = [min(SLOTS[i], chunks - 1) if i < len(SLOTS) else chunks - 1 for i in range(len(later))]

    @pl.loop(0, chunks)
    def _(j):
        w_copy(j).wait()
        part[j] = lax.dot_general(
            up_all[...], w_all[j], (((1,), (1,)), ((), ())), preferred_element_type=jnp.float32
        ).astype(part.dtype)
        for way in range(2):
            p = place[way]

            @pl.when(p == 0)
            def _():
                if n >= 3:
                    rs_hop(way, j, n - 1)

            @pl.when((p > 0) & (p <= n - 3) & (j >= LAG))
            def _():
                rs_hop(way, j - LAG, n - 1)
        for (s, c), slot in zip(later, slot_of):
            if slot < chunks - 1:
                @pl.when(j == slot)
                def _():
                    ag_pass(s, c)

    for (s, c), slot in zip(later, slot_of):
        if slot >= chunks - 1:
            ag_pass(s, c)

    @pl.loop(max(chunks - LAG, 0), chunks)
    def _(j):
        for way in range(2):
            @pl.when((place[way] > 0) & (place[way] <= n - 3))
            def _():
                rs_hop(way, j, n - 1)

    for e in range(n - 2, 1, -1):
        @pl.loop(0, chunks)
        def _(j):
            for way in range(2):
                @pl.when(place[way] <= e - 2)
                def _():
                    rs_hop(way, j, e)

    for j in range(chunks):
        columns = pl.ds(j * unit, unit)
        own[:, columns] = part_at(j, z)[...]
        for way, out in ((0, to_right), (1, to_left)):
            p = place[way]
            b = jnp.clip(z + (1 - 2 * way), 0, n - 1)

            @pl.when((p > 0) & (p < n - 1))
            def _():
                out[:, columns] = rs_add(way, j, b)

            @pl.when((p == 0) | (p == n - 1))
            def _():
                out[:, columns] = part_at(j, b)[...]

    for way in range(2):
        for s in range(1, n):
            @pl.when((place[way] >= s) & ((place[way] == n - 1) | (s == n - 1)))
            def _():
                for c in range(HALVES):
                    ag_arrive(way, s, c)

    for a in range(depth_n):
        for b in range(pair_n):
            core_copy(a, b, source(a, b, core)).wait_send()
            if a and not b:
                x_copy(a, mine).wait_send()
            if b and not a:
                y_copy(b, mine).wait_send()
            if a and b:
                turn_copy(0, a, b, source(a, 0, core)).wait_send()
                turn_copy(1, a, b, source(0, b, core)).wait_send()
    for way in range(2):
        for s in range(1, n):
            @pl.when((place[way] >= s - 1) & (place[way] < n - 1))
            def _():
                for c in range(HALVES):
                    ag_copy(way, s, c).wait_send()
        for e in range(2, n):
            @pl.when(place[way] <= e - 2)
            def _():
                @pl.loop(0, chunks)
                def _(j):
                    rs_copy(way, j, block_of(way, e)).wait_send()
    keep_hid.wait()
    keep_up.wait()


def exchange(hidden, upstream, weight, n, depth_n, row_n):
    rows, units = hidden.shape
    up_rows, features = upstream.shape
    tokens = rows * n
    chunks = 7 if units % (7 * 128) == 0 else 1
    unit = units // chunks
    pair_n = row_n // 2
    half = jnp.bfloat16
    hbm = pl.BlockSpec(memory_space=pl.ANY)
    vmem = pl.BlockSpec(memory_space=pltpu.VMEM)
    small = jax.ShapeDtypeStruct((rows, units), half)
    dma = pltpu.SemaphoreType.DMA
    return pl.pallas_call(
        functools.partial(exchange_kernel, (n, depth_n, row_n, chunks)),
        out_shape=[
            jax.ShapeDtypeStruct((tokens, units), half),
            jax.ShapeDtypeStruct((tokens, features), half),
            small, small, small,
        ],
        in_specs=[hbm, hbm, hbm],
        out_specs=[hbm, hbm, vmem, vmem, vmem],
        scratch_shapes=[
            pltpu.VMEM((tokens, features), half),
            pltpu.VMEM((chunks, unit, features), half),
            pltpu.VMEM((chunks, tokens, unit), half),
            pltpu.VMEM((2, chunks, n, rows, unit), half),
            pltpu.VMEM((rows, units), half),
            dma, dma, dma((chunks,)), dma,
            dma((depth_n,)), dma((depth_n,)), dma((pair_n,)), dma((pair_n,)),
            dma((2, depth_n, pair_n)), dma((2, depth_n, pair_n)), dma((depth_n, pair_n)), dma((depth_n, pair_n)),
            dma((2, n - 1, HALVES)), dma((2, n - 1, HALVES)),
            dma((2, chunks, n)), dma((2, chunks, n)),
        ],
        compiler_params=pltpu.CompilerParams(
            collective_id=0, has_side_effects=True, vmem_limit_bytes=VMEM_BYTES),
        cost_estimate=pl.CostEstimate(
            flops=2 * tokens * units * features, bytes_accessed=2 * units * features, transcendentals=0),
    )(hidden, upstream, weight)


def weight_kernel(scale, hid, up, out):
    width = out.shape[1]
    step = 512 if width % 512 == 0 else 128
    for first in range(0, width, step):
        columns = slice(first, first + step)
        summed = lax.dot_general(
            hid[...], up[:, columns], (((0,), (0,)), ((), ())), preferred_element_type=jnp.float32)
        out[:, columns] = (summed * scale).astype(out.dtype)


def weight_gradient(hidden_all, upstream_all):
    tokens, units = hidden_all.shape
    features = upstream_all.shape[1]
    unit = 512 if units % 512 == 0 else 128
    return pl.pallas_call(
        functools.partial(weight_kernel, 1.0 / math.sqrt(tokens)),
        grid=(units // unit,),
        in_specs=[
            pl.BlockSpec((tokens, unit), lambda i: (0, i)),
            pl.BlockSpec((tokens, features), lambda i: (0, 0)),
        ],
        out_specs=pl.BlockSpec((unit, features), lambda i: (i, 0)),
        out_shape=jax.ShapeDtypeStruct((units, features), jnp.bfloat16),
        compiler_params=pltpu.CompilerParams(vmem_limit_bytes=VMEM_BYTES),
        cost_estimate=pl.CostEstimate(
            flops=2 * tokens * units * features, bytes_accessed=2 * units * features, transcendentals=0),
    )(hidden_all, upstream_all)


def local(sizes, hidden, upstream, weight):
    n, depth_n, row_n = sizes
    hidden_all, upstream_all, own, to_right, to_left = exchange(hidden, upstream, weight, n, depth_n, row_n)
    from_left = lax.ppermute(to_right, "col", [(i, i + 1) for i in range(n - 1)])
    from_right = lax.ppermute(to_left, "col", [(i + 1, i) for i in range(n - 1)])
    weight_grad = weight_gradient(hidden_all, upstream_all)
    wide = jnp.float32
    input_grad = (own.astype(wide) + from_left.astype(wide) + from_right.astype(wide)).astype(jnp.bfloat16)
    return (input_grad, weight_grad)


def solution(mesh):
    sizes = (mesh.shape["col"], mesh.shape["depth"], mesh.shape["row"])
    in_specs = (P("col", ("depth", "row")), P(("depth", "row"), "col"), P(("depth", "row"), "col"))
    out_specs = (P("col", ("depth", "row")), P(("depth", "row"), "col"))
    return jax.shard_map(
        functools.partial(local, sizes), mesh=mesh, in_specs=in_specs, out_specs=out_specs, check_vma=False)
```

```python
import functools
import math

import jax
import jax.numpy as jnp
from jax import lax
from jax.experimental import pallas as pl
from jax.experimental.pallas import tpu as pltpu
from jax.sharding import PartitionSpec as P

MESH = pl.DeviceIdType.MESH
HALVES = 2
LAG = 2
SLOTS = (0, 4)
VMEM_BYTES = 60 * 1024 * 1024


def exchange_kernel(
    sizes, hid, up, w, hall, uall, own, to_right, to_left,
    up_all, w_all, part, got, hid_own,
    up_local, hid_local, w_sem, out_sem,
    x_send, x_recv, y_send, y_recv, turn_send, turn_recv, core_send, core_recv,
    ag_send, ag_recv, rs_send, rs_recv,
):
    n, depth_n, row_n, chunks = sizes
    pair_n = row_n // 2
    rows = hid.shape[0]
    up_rows = up.shape[0]
    unit = part.shape[2]
    half = rows // HALVES
    depth, row, z = lax.axis_index("depth"), lax.axis_index("row"), lax.axis_index("col")
    core, pair = lax.rem(row, 2), lax.div(row, 2)

    def plane(a, b, c):
        return (lax.rem(depth + a, depth_n), 2 * lax.rem(pair + b, pair_n) + c, z)

    def source(a, b, c):
        return lax.rem(depth - a + depth_n, depth_n) * row_n + 2 * lax.rem(pair - b + pair_n, pair_n) + c

    def line(way):
        return (depth, row, jnp.clip(z + (1 - 2 * way), 0, n - 1))

    place = (z, n - 1 - z)

    def block_of(way, e):
        return e if way == 0 else n - 1 - e

    barrier = pltpu.get_barrier_semaphore()
    peers = [plane(a, 0, core) for a in range(1, depth_n)]
    peers += [plane(0, b, core) for b in range(1, pair_n)]
    peers += [plane(0, 0, 1 - core)]
    for peer in peers:
        pl.semaphore_signal(barrier, inc=1, device_id=peer, device_id_type=MESH)
    for way in range(2):
        @pl.when(place[way] < n - 1)
        def _():
            pl.semaphore_signal(barrier, inc=1, device_id=line(way), device_id_type=MESH)
    near = jnp.where(z > 0, 1, 0) + jnp.where(z < n - 1, 1, 0)
    pl.semaphore_wait(barrier, len(peers) + near)

    def up_at(i, first=0, count=None):
        count = up_rows if count is None else count
        return up_all.at[pl.ds(pl.multiple_of(i * up_rows + first, count), count), :]

    def remote(src, dst, send, recv, peer):
        return pltpu.make_async_remote_copy(
            src_ref=src, dst_ref=dst, send_sem=send, recv_sem=recv, device_id=peer, device_id_type=MESH)

    def x_copy(a, i):
        return remote(up, up_at(i), x_send.at[a], x_recv.at[a], plane(a, 0, core))

    def y_copy(b, i):
        return remote(up, up_at(i), y_send.at[b], y_recv.at[b], plane(0, b, core))

    def turn_copy(part_of, a, b, i):
        piece = up_at(i, part_of * (up_rows // 2), up_rows // 2)
        peer = plane(0, b, core) if part_of == 0 else plane(a, 0, core)
        return remote(piece, piece, turn_send.at[part_of, a, b], turn_recv.at[part_of, a, b], peer)

    def core_copy(a, b, i):
        src = up if a == 0 and b == 0 else up_at(i)
        return remote(src, up_at(i), core_send.at[a, b], core_recv.at[a, b], plane(0, 0, 1 - core))

    def hid_rows(ref, b, c):
        return ref.at[pl.ds(pl.multiple_of(b * rows + c * half, half), half), :]

    def ag_copy(way, s, c):
        b = jnp.clip(z - (1 - 2 * way) * (s - 1), 0, n - 1)
        src = hid.at[pl.ds(c * half, half), :] if s == 1 else hid_rows(hall, b, c)
        return pltpu.make_async_remote_copy(
            src_ref=src, dst_ref=hid_rows(hall, b, c),
            send_sem=ag_send.at[way, s - 1, c], recv_sem=ag_recv.at[way, s - 1, c],
            device_id=line(way), device_id_type=MESH)

    def ag_arrive(way, s, c):
        b = jnp.clip(z - (1 - 2 * way) * s, 0, n - 1)
        pltpu.make_async_remote_copy(
            src_ref=hid_rows(hall, b, c), dst_ref=hid_rows(hall, b, c),
            send_sem=ag_send.at[way, s - 1, c], recv_sem=ag_recv.at[way, s - 1, c],
            device_id=line(way), device_id_type=MESH).wait_recv()

    def ag_pass(s, c):
        for way in range(2):
            @pl.when((place[way] >= s) & (place[way] < n - 1))
            def _():
                ag_arrive(way, s, c)
                ag_copy(way, s + 1, c).start()

    mine = source(0, 0, core)
    for a in range(1, depth_n):
        x_copy(a, mine).start()
    for b in range(1, pair_n):
        y_copy(b, mine).start()
    core_copy(0, 0, mine).start()
    for c in range(HALVES):
        for way in range(2):
            @pl.when(place[way] < n - 1)
            def _():
                ag_copy(way, 1, c).start()
    own_up = pltpu.make_async_copy(up, up_at(mine), up_local)
    own_up.start()
    own_hid = pltpu.make_async_copy(hid, hid_own, hid_local)
    own_hid.start()

    def w_copy(j):
        return pltpu.make_async_copy(
            w.at[pl.ds(pl.multiple_of(j * unit, unit), unit), :], w_all.at[j], w_sem.at[j])

    for j in range(chunks):
        w_copy(j).start()

    own_hid.wait()
    keep_hid = pltpu.make_async_copy(
        hid_own, hall.at[pl.ds(pl.multiple_of(z * rows, rows), rows), :], hid_local)
    keep_hid.start()
    for a in range(1, depth_n):
        i = source(a, 0, core)
        x_copy(a, i).wait_recv()
        for b in range(1, pair_n):
            turn_copy(0, a, b, i).start()
        core_copy(a, 0, i).start()
    for b in range(1, pair_n):
        i = source(0, b, core)
        y_copy(b, i).wait_recv()
        for a in range(1, depth_n):
            turn_copy(1, a, b, i).start()
        core_copy(0, b, i).start()
    for c in range(HALVES - 1):
        ag_pass(1, c)
    for a in range(1, depth_n):
        for b in range(1, pair_n):
            i = source(a, b, core)
            turn_copy(0, a, b, i).wait_recv()
            turn_copy(1, a, b, i).wait_recv()
            core_copy(a, b, i).start()
    own_up.wait()
    for a in range(depth_n):
        for b in range(pair_n):
            core_copy(a, b, source(a, b, 1 - core)).wait_recv()
    keep_up = pltpu.make_async_copy(up_all, uall, out_sem)
    keep_up.start()

    def part_at(j, b):
        return part.at[j, pl.ds(pl.multiple_of(b * rows, rows), rows), :]

    def rs_copy(way, j, b):
        return pltpu.make_async_remote_copy(
            src_ref=part_at(j, b), dst_ref=got.at[way, j, b],
            send_sem=rs_send.at[way, j, b], recv_sem=rs_recv.at[way, j, b],
            device_id=line(way), device_id_type=MESH)

    def rs_add(way, j, b):
        rs_copy(way, j, b).wait_recv()
        return (part_at(j, b)[...].astype(jnp.float32) + got[way, j, b].astype(jnp.float32)).astype(part.dtype)

    def rs_hop(way, j, e):
        b = block_of(way, e)

        @pl.when(place[way] > 0)
        def _():
            part_at(j, b)[...] = rs_add(way, j, b)
        rs_copy(way, j, b).start()

    later = [(1, HALVES - 1)] + [(s, c) for s in range(2, n - 1) for c in range(HALVES)]
    slot_of = [min(SLOTS[i], chunks - 1) if i < len(SLOTS) else chunks - 1 for i in range(len(later))]

    @pl.loop(0, chunks)
    def _(j):
        w_copy(j).wait()
        part[j] = lax.dot_general(
            up_all[...], w_all[j], (((1,), (1,)), ((), ())), preferred_element_type=jnp.float32
        ).astype(part.dtype)
        for way in range(2):
            p = place[way]

            @pl.when(p == 0)
            def _():
                if n >= 3:
                    rs_hop(way, j, n - 1)

            @pl.when((p > 0) & (p <= n - 3) & (j >= LAG))
            def _():
                rs_hop(way, j - LAG, n - 1)
        for (s, c), slot in zip(later, slot_of):
            if slot < chunks - 1:
                @pl.when(j == slot)
                def _():
                    ag_pass(s, c)

    for (s, c), slot in zip(later, slot_of):
        if slot >= chunks - 1:
            ag_pass(s, c)

    @pl.loop(max(chunks - LAG, 0), chunks)
    def _(j):
        for way in range(2):
            @pl.when((place[way] > 0) & (place[way] <= n - 3))
            def _():
                rs_hop(way, j, n - 1)

    for e in range(n - 2, 1, -1):
        @pl.loop(0, chunks)
        def _(j):
            for way in range(2):
                @pl.when(place[way] <= e - 2)
                def _():
                    rs_hop(way, j, e)

    for j in range(chunks):
        columns = pl.ds(j * unit, unit)
        own[:, columns] = part_at(j, z)[...]
        for way, out in ((0, to_right), (1, to_left)):
            p = place[way]
            b = jnp.clip(z + (1 - 2 * way), 0, n - 1)

            @pl.when((p > 0) & (p < n - 1))
            def _():
                out[:, columns] = rs_add(way, j, b)

            @pl.when((p == 0) | (p == n - 1))
            def _():
                out[:, columns] = part_at(j, b)[...]

    for way in range(2):
        for s in range(1, n):
            @pl.when((place[way] >= s) & ((place[way] == n - 1) | (s == n - 1)))
            def _():
                for c in range(HALVES):
                    ag_arrive(way, s, c)

    for a in range(depth_n):
        for b in range(pair_n):
            core_copy(a, b, source(a, b, core)).wait_send()
            if a and not b:
                x_copy(a, mine).wait_send()
            if b and not a:
                y_copy(b, mine).wait_send()
            if a and b:
                turn_copy(0, a, b, source(a, 0, core)).wait_send()
                turn_copy(1, a, b, source(0, b, core)).wait_send()
    for way in range(2):
        for s in range(1, n):
            @pl.when((place[way] >= s - 1) & (place[way] < n - 1))
            def _():
                for c in range(HALVES):
                    ag_copy(way, s, c).wait_send()
        for e in range(2, n):
            @pl.when(place[way] <= e - 2)
            def _():
                @pl.loop(0, chunks)
                def _(j):
                    rs_copy(way, j, block_of(way, e)).wait_send()
    keep_hid.wait()
    keep_up.wait()


def exchange(hidden, upstream, weight, n, depth_n, row_n):
    rows, units = hidden.shape
    up_rows, features = upstream.shape
    tokens = rows * n
    chunks = 7 if units % (7 * 128) == 0 else 1
    unit = units // chunks
    pair_n = row_n // 2
    half = jnp.bfloat16
    hbm = pl.BlockSpec(memory_space=pl.ANY)
    vmem = pl.BlockSpec(memory_space=pltpu.VMEM)
    small = jax.ShapeDtypeStruct((rows, units), half)
    dma = pltpu.SemaphoreType.DMA
    return pl.pallas_call(
        functools.partial(exchange_kernel, (n, depth_n, row_n, chunks)),
        out_shape=[
            jax.ShapeDtypeStruct((tokens, units), half),
            jax.ShapeDtypeStruct((tokens, features), half),
            small, small, small,
        ],
        in_specs=[hbm, hbm, hbm],
        out_specs=[hbm, hbm, vmem, vmem, vmem],
        scratch_shapes=[
            pltpu.VMEM((tokens, features), half),
            pltpu.VMEM((chunks, unit, features), half),
            pltpu.VMEM((chunks, tokens, unit), half),
            pltpu.VMEM((2, chunks, n, rows, unit), half),
            pltpu.VMEM((rows, units), half),
            dma, dma, dma((chunks,)), dma,
            dma((depth_n,)), dma((depth_n,)), dma((pair_n,)), dma((pair_n,)),
            dma((2, depth_n, pair_n)), dma((2, depth_n, pair_n)), dma((depth_n, pair_n)), dma((depth_n, pair_n)),
            dma((2, n - 1, HALVES)), dma((2, n - 1, HALVES)),
            dma((2, chunks, n)), dma((2, chunks, n)),
        ],
        compiler_params=pltpu.CompilerParams(
            collective_id=0, has_side_effects=True, vmem_limit_bytes=VMEM_BYTES),
        cost_estimate=pl.CostEstimate(
            flops=2 * tokens * units * features, bytes_accessed=2 * units * features, transcendentals=0),
    )(hidden, upstream, weight)


def weight_kernel(scale, hid, up, out):
    width = out.shape[1]
    step = 512 if width % 512 == 0 else 128
    for first in range(0, width, step):
        columns = slice(first, first + step)
        summed = lax.dot_general(
            hid[...], up[:, columns], (((0,), (0,)), ((), ())), preferred_element_type=jnp.float32)
        out[:, columns] = (summed * scale).astype(out.dtype)


def weight_gradient(hidden_all, upstream_all):
    tokens, units = hidden_all.shape
    features = upstream_all.shape[1]
    unit = 512 if units % 512 == 0 else 128
    return pl.pallas_call(
        functools.partial(weight_kernel, 1.0 / math.sqrt(tokens)),
        grid=(units // unit,),
        in_specs=[
            pl.BlockSpec((tokens, unit), lambda i: (0, i)),
            pl.BlockSpec((tokens, features), lambda i: (0, 0)),
        ],
        out_specs=pl.BlockSpec((unit, features), lambda i: (i, 0)),
        out_shape=jax.ShapeDtypeStruct((units, features), jnp.bfloat16),
        compiler_params=pltpu.CompilerParams(vmem_limit_bytes=VMEM_BYTES),
        cost_estimate=pl.CostEstimate(
            flops=2 * tokens * units * features, bytes_accessed=2 * units * features, transcendentals=0),
    )(hidden_all, upstream_all)


def local(sizes, hidden, upstream, weight):
    n, depth_n, row_n = sizes
    hidden_all, upstream_all, own, to_right, to_left = exchange(hidden, upstream, weight, n, depth_n, row_n)
    from_left = lax.ppermute(to_right, "col", [(i, i + 1) for i in range(n - 1)])
    from_right = lax.ppermute(to_left, "col", [(i + 1, i) for i in range(n - 1)])
    weight_grad = weight_gradient(hidden_all, upstream_all)
    wide = jnp.float32
    input_grad = (own.astype(wide) + from_left.astype(wide) + from_right.astype(wide)).astype(jnp.bfloat16)
    return (input_grad, weight_grad)


def solution(mesh):
    sizes = (mesh.shape["col"], mesh.shape["depth"], mesh.shape["row"])
    in_specs = (P("col", ("depth", "row")), P(("depth", "row"), "col"), P(("depth", "row"), "col"))
    out_specs = (P("col", ("depth", "row")), P(("depth", "row"), "col"))
    return jax.shard_map(
        functools.partial(local, sizes), mesh=mesh, in_specs=in_specs, out_specs=out_specs, check_vma=False)
```
